32 devices in a mesh: groups: 1, ep: 8 (over z, y), tp: 4 (over x, core).
Axes of the slice: x: 2, y: 2, z: 4, core: 2. Of those that a mesh axis runs over, the one named last changes fastest.
Arguments:
- queries: bfloat16 [1024, 4096], P(('groups', 'ep', 'tp')), may hold values from -6.5 to 6.5
- cache_keys: bfloat16 [1024, 8, 32, 128], P(('groups', 'ep', 'tp')), may hold values from -6.5 to 6.5
- cache_values: bfloat16 [1024, 8, 32, 128], P(('groups', 'ep', 'tp')), may hold values from -6 to 6
- new_keys: bfloat16 [1024, 4, 128], P(('groups', 'ep', 'tp')), may hold values from -6.5 to 6.5
- new_values: bfloat16 [1024, 4, 128], P(('groups', 'ep', 'tp')), may hold values from -6 to 6
- lengths: int32 [1024], P(('groups', 'ep', 'tp')), may hold values from 1 to 64, as said below
- residual: bfloat16 [1024, 4096], P(('groups', 'ep'), 'tp'), may hold values from -12 to 12
- norm_gain: bfloat16 [4096], replicated, may hold values from 0.099609375 to 1.8984375
- routes: int32 [1024, 8], P(('groups', 'ep')), may hold values from 0 to 15, all different within a row; in each aligned block of 64 rows (0 to 63, 64 to 127, ...) at most 64 rows name the same one
- route_weights: float32 [1024, 8], P(('groups', 'ep')), may hold values from 0.05 to 0.3
- expert_slot: int32 [16], replicated, may hold values from 0 to 15, each once
- gate_halves: bfloat16 [32, 4096, 384], P(('ep', 'tp')), may hold values from -0.09375 to 0.09375
- up_halves: bfloat16 [32, 4096, 384], P(('ep', 'tp')), may hold values from -0.09375 to 0.09375
- down_halves: bfloat16 [32, 384, 4096], P(('ep', 'tp')), may hold values from -0.21875 to 0.21875
Outputs:
- mixed: bfloat16 [1024, 4096], P(('groups', 'ep'), 'tp')
The draws below stay inside these ranges and needn't reach their ends.
Inputs may be any that keep to these rules, and one draw needn't show every extreme that they name: Rows of one index of ep have cache lengths up to a bound of their own; the longest bound is 64, reached by some row. `routes`: among the rows of one micro-batch of one index of ep (aligned blocks of 64 rows) no expert is named more than 64 times. `expert_slot`: each slot holds one expert.
All inputs are finite; a program needn't handle non-finite values.
Results may differ from the reference program's by a relative error of at most 0.015.
Values may be sent and summed in bfloat16 or wider, within the bound.
A program may use at most 128 MiB of HBM per device.

```python
import math
import jax
import jax.numpy as jnp
import numpy as np
from jax import lax

D = 4096
QH = 32
KVH = 4
HD = 128
H = 768
TOPK = 8
LMAX = 64
MB_ROWS = 64
ROWS_DEV = 128
ROWS = 1024
EXPERTS = 16
CAP = 64
N_EP = 8


def draw_queries(key, part):
    key = jax.random.fold_in(key, 1)
    base_draw = jnp.clip(jax.random.normal(key, (ROWS, QH, HD), jnp.float32), -5.0, 5.0)
    return base_draw.reshape(ROWS, QH * HD).astype(jnp.bfloat16)


def draw_new_keys(key, part):
    key = jax.random.fold_in(key, 2)
    base_draw = jnp.clip(jax.random.normal(key, (ROWS, KVH, HD), jnp.float32), -5.0, 5.0)
    return base_draw.astype(jnp.bfloat16)


def draw_cache_keys(key, part):
    key = jax.random.fold_in(key, 3)
    base_draw = jnp.clip(jax.random.normal(key, (ROWS, 2 * KVH, LMAX // 2, HD), jnp.float32), -5.0, 5.0)
    return base_draw.astype(jnp.bfloat16)


def draw_lengths(key, part):
    key = jax.random.fold_in(key, 4)
    bound_key, row_key = jax.random.split(key)
    block_count = ROWS // ROWS_DEV
    bounds = jax.random.randint(bound_key, (block_count,), LMAX // 4, LMAX + 1)
    bounds = bounds.at[0].set(LMAX)
    per_row = jnp.repeat(bounds, ROWS_DEV)
    row_draw = jax.random.randint(row_key, (ROWS,), 1, per_row + 1)
    leading = jnp.arange(ROWS) % ROWS_DEV == 0
    return jnp.where(leading, per_row, row_draw).astype(jnp.int32)


def draw_residual(key, part):
    key = jax.random.fold_in(key, 5)
    noise_key, row_key, column_key = jax.random.split(key, 3)
    row_scale = 10.0 ** (0.6 * jax.random.uniform(row_key, (ROWS, 1)))
    column_ramp = jnp.arange(D, dtype=jnp.float32) / (D - 1)
    column_scale = 10.0 ** (0.25 * jax.random.uniform(column_key, (D,)) + 0.24 * column_ramp)
    noise_draw = jnp.clip(jax.random.normal(noise_key, (ROWS, D), jnp.float32), -4.0, 4.0)
    return (0.04 * noise_draw * row_scale * column_scale[None, :]).astype(jnp.bfloat16)


def shard_levels(stream_key, shape, cuts, smallest, top_value):
    level = 1.0
    for axis_at, shards_of in cuts:
        steps = jax.random.uniform(jax.random.fold_in(jax.random.fold_in(stream_key, 6), axis_at), (shards_of,), jnp.float32, smallest / len(cuts), top_value / len(cuts))
        level = level * jnp.repeat(jnp.exp(steps), shape[axis_at] // shards_of).reshape((-1,) + (1,) * (len(shape) - 1 - axis_at))
    return level


def assign_block(own_key, own, number, rows, amount, top, most, slope):
    ranking = jax.random.permutation(own_key, amount)
    packed, usual = load_shares(amount, rows * top, most, slope, True), load_shares(amount, rows * top, most, slope, False)
    places = jnp.arange(amount)

    def named(tallies, offset_by):
        used = int((tallies > 0).sum())
        fixed = max(1, used // 4)
        shifted = fixed + (places - fixed + offset_by * (used - fixed)) % max(1, amount - fixed)
        return jnp.zeros((amount,), jnp.int32).at[ranking[jnp.where(places < fixed, places, shifted)]].set(jnp.asarray(tallies, jnp.int32))

    tallies = jnp.where(number % 4 == 0, named(packed, number // 4), named(usual, number - number // 4 - 1))
    mixed = jax.random.permutation(jax.random.fold_in(own, 3), amount)
    source_of, sink = mixed[0:amount // 2 * 2:2], mixed[1:amount // 2 * 2:2]
    slack = jnp.minimum(tallies[source_of] - 1, most - tallies[sink]) // 2
    slack = jnp.where((source_of == ranking[0]) | (sink == ranking[0]) | (tallies[sink] == 0), 0, jnp.maximum(slack, 0))
    shifted = jax.random.randint(jax.random.fold_in(own, 4), (amount // 2,), 0, 1 << 20) % (slack + 1)
    tallies = tallies.at[source_of].add(-shifted).at[sink].add(shifted)
    items = jnp.searchsorted(jnp.cumsum(tallies), jnp.arange(rows * top), side="right").astype(jnp.int32)
    table = items.reshape(top, rows).T
    table = table[jax.random.permutation(jax.random.fold_in(own, 1), rows)]
    offset_by = jax.random.randint(jax.random.fold_in(own, 2), (rows, 1), 0, top)
    return jnp.take_along_axis(table, (jnp.arange(top)[None, :] + offset_by) % top, axis=1)


def load_shares(number_of, total, most, slope, full):
    portions = [(1 << 20) // math.isqrt(standing ** slope) + 1 for standing in range(1, number_of + 1)]
    largest = most if full else min(most, max(-(-total // number_of), total * portions[0] // sum(portions)))
    least = 1 if total - largest >= number_of - 1 else 0
    given, surplus = [largest] + [least] * (number_of - 1), total - largest - least * (number_of - 1)
    while surplus > 0:
        free = [i for i in range(1, number_of) if given[i] < largest] or [i for i in range(1, number_of) if given[i] < most]
        whole, budget = sum([portions[i] for i in free]), surplus
        for i in free:
            more = min(most - given[i], max(1, budget * portions[i] // whole), surplus)
            given[i] = given[i] + more
            surplus = surplus - more
    return np.array(given)


def bell_draw(stream_key, shape, spread, most, cuts=(), held_as=jnp.bfloat16):
    gain = shard_levels(stream_key, shape, cuts, -0.22, 0.18) if cuts else 1.0
    drawn = jax.random.normal(stream_key, shape, jnp.float32) * spread * gain
    return jnp.minimum(jnp.maximum(drawn, -most), most).astype(held_as)


def setup_inputs(seed: int = 0, part: int = 0) -> dict:
    key_of = jax.random.split(jax.random.key(seed), 15)
    part_splits = jax.random.split(jax.random.fold_in(key_of[14], part), 15)
    queries = draw_queries(jax.random.fold_in(jax.random.fold_in(key_of[14], part), 71), part)
    cache_keys = draw_cache_keys(jax.random.fold_in(jax.random.fold_in(key_of[14], part), 71), part)
    cache_values = bell_draw(part_splits[2], (ROWS, 2 * KVH, LMAX // 2, HD), 1.0, 6.0, ((0, 32),))
    new_keys = draw_new_keys(jax.random.fold_in(jax.random.fold_in(key_of[14], part), 71), part)
    new_values = bell_draw(part_splits[4], (ROWS, KVH, HD), 1.0, 6.0, ((0, 32),))
    lengths = draw_lengths(jax.random.fold_in(jax.random.fold_in(key_of[14], part), 71), part)
    residual = draw_residual(jax.random.fold_in(jax.random.fold_in(key_of[14], part), 71), part)
    norm_gain = jnp.clip(1.0 + 0.18 * jax.random.normal(key_of[7], (D,), jnp.float32), 0.099609375, 1.8984375).astype(jnp.bfloat16)
    routes_keys = jax.random.split(jax.random.fold_in(part_splits[8], 1), ROWS // MB_ROWS)
    routes_turns = jax.random.permutation(jax.random.fold_in(part_splits[8], 3), ROWS // MB_ROWS)
    routes = jax.vmap(lambda own, number: assign_block(jax.random.fold_in(part_splits[8], 2), own, number, MB_ROWS, EXPERTS, TOPK, CAP, 2))(routes_keys, routes_turns).reshape((ROWS, TOPK))
    route_weights = jnp.clip(0.05 + 0.25 * jax.random.uniform(part_splits[9], (ROWS, TOPK), jnp.float32) ** shard_levels(part_splits[9], (ROWS, TOPK), ((0, 8),), -0.2, 0.2), 0.05, 0.3)
    expert_slot = jax.random.permutation(key_of[10], EXPERTS).astype(jnp.int32)
    gate_halves = bell_draw(key_of[11], (2 * EXPERTS, D, H // 2), D ** -0.5, 0.09375, ((0, 32),))
    up_halves = bell_draw(key_of[12], (2 * EXPERTS, D, H // 2), D ** -0.5, 0.09375, ((0, 32),))
    down_halves = bell_draw(key_of[13], (2 * EXPERTS, H // 2, D), H ** -0.5, 0.21875, ((0, 32),))
    return {"queries": queries, "cache_keys": cache_keys, "cache_values": cache_values, "new_keys": new_keys, "new_values": new_values, "lengths": lengths, "residual": residual, "norm_gain": norm_gain, "routes": routes, "route_weights": route_weights, "expert_slot": expert_slot, "gate_halves": gate_halves, "up_halves": up_halves, "down_halves": down_halves}


def attend_block(block):
    query, key_cache, value_cache, fresh_key, fresh_value, length = block
    row_count = query.shape[0]
    group_size = QH // KVH
    query_f = query.reshape(row_count, KVH, group_size, HD).astype(jnp.float32)
    key_f = key_cache.reshape(row_count, KVH, LMAX, HD).astype(jnp.float32)
    value_f = value_cache.reshape(row_count, KVH, LMAX, HD).astype(jnp.float32)
    score_scale = 1.0 / jnp.sqrt(jnp.float32(HD))
    scores = jnp.einsum('rgqd,rgpd->rgqp', query_f, key_f) * score_scale
    fresh_score = jnp.einsum('rgqd,rgd->rgq', query_f, fresh_key.astype(jnp.float32)) * score_scale
    is_valid = jnp.arange(LMAX, dtype=jnp.int32)[None, :] < length[:, None]
    scores = jnp.where(is_valid[:, None, None, :], scores, -jnp.inf)
    every_score = jnp.concatenate([scores, fresh_score[:, :, :, None]], axis=3)
    weights = jax.nn.softmax(every_score, axis=3)
    every_value = jnp.concatenate([value_f, fresh_value.astype(jnp.float32)[:, :, None, :]], axis=2)
    output = jnp.einsum('rgqp,rgpd->rgqd', weights, every_value)
    return output.reshape(row_count, D)

def reference(queries, cache_keys, cache_values, new_keys, new_values, lengths, residual, norm_gain, routes, route_weights, expert_slot, gate_halves, up_halves, down_halves):
    block_count = ROWS // ROWS_DEV
    blocks = (queries.reshape(block_count, ROWS_DEV, D), cache_keys.reshape(block_count, ROWS_DEV, 2 * KVH, LMAX // 2, HD), cache_values.reshape(block_count, ROWS_DEV, 2 * KVH, LMAX // 2, HD), new_keys.reshape(block_count, ROWS_DEV, KVH, HD), new_values.reshape(block_count, ROWS_DEV, KVH, HD), lengths.reshape(block_count, ROWS_DEV))
    attention = lax.map(attend_block, blocks).reshape(ROWS, D)
    stream = (residual.astype(jnp.float32) + attention).astype(jnp.bfloat16)
    stream_f = stream.astype(jnp.float32)
    mean_square = lax.optimization_barrier(jnp.mean(stream_f * stream_f, axis=1, keepdims=True))
    normed = (stream_f * lax.rsqrt(mean_square + 1e-06) * norm_gain.astype(jnp.float32)[None, :]).astype(jnp.bfloat16)
    limit = min(ROWS, 2 * N_EP * CAP)
    slot_ids = jnp.arange(EXPERTS, dtype=jnp.int32)

    def add_slot(mixture, slot):
        expert = jnp.sum(jnp.where(expert_slot == slot, slot_ids, 0)).astype(jnp.int32)
        is_hit = routes == expert
        row_weight = lax.optimization_barrier(jnp.sum(jnp.where(is_hit, route_weights, 0.0), axis=1))
        chosen = jnp.any(is_hit, axis=1)
        order = jnp.argsort(jnp.where(chosen, 0, 1).astype(jnp.int32), stable=True)[:limit].astype(jnp.int32)
        inputs = normed[order]
        pieces = jnp.zeros((limit, D), jnp.float32)
        for half_index in range(2):
            half_row = (2 * slot + half_index).astype(jnp.int32)
            gate_half = lax.dynamic_index_in_dim(gate_halves, half_row, 0, keepdims=False)
            up_half = lax.dynamic_index_in_dim(up_halves, half_row, 0, keepdims=False)
            down_half = lax.dynamic_index_in_dim(down_halves, half_row, 0, keepdims=False)
            gate_out = jnp.dot(inputs, gate_half, preferred_element_type=jnp.float32)
            up_out = jnp.dot(inputs, up_half, preferred_element_type=jnp.float32)
            hidden = (jax.nn.silu(gate_out) * up_out).astype(jnp.bfloat16)
            piece = jnp.dot(hidden, down_half, preferred_element_type=jnp.float32).astype(jnp.bfloat16)
            piece = lax.optimization_barrier(piece)
            pieces = pieces + piece.astype(jnp.float32)
        factor = jnp.where(chosen[order], row_weight[order], 0.0).astype(jnp.float32)
        return (mixture.at[order].add(pieces * factor[:, None]), None)
    mixture, unused = lax.scan(add_slot, jnp.zeros((ROWS, D), jnp.float32), slot_ids)
    return (stream_f + mixture).astype(jnp.bfloat16)
```

```python
import functools

import jax
import jax.numpy as jnp
from jax import lax
from jax.experimental import pallas as pl
from jax.experimental.pallas import tpu as pltpu
from jax.sharding import PartitionSpec as P

EPSILON = 1e-06


def attend(queries, cache_keys, cache_values, new_keys, new_values, lengths):
    row_count = queries.shape[0]
    kv_heads = new_keys.shape[1]
    head_dim = new_keys.shape[2]
    group_size = queries.shape[1] // (kv_heads * head_dim)
    span = cache_keys.shape[2] * 2
    query_f = queries.reshape(row_count, kv_heads, group_size, head_dim).astype(jnp.float32)
    key_f = cache_keys.reshape(row_count, kv_heads, span, head_dim).astype(jnp.float32)
    value_f = cache_values.reshape(row_count, kv_heads, span, head_dim).astype(jnp.float32)
    score_scale = 1.0 / jnp.sqrt(jnp.float32(head_dim))
    scores = jnp.einsum("rgqd,rgpd->rgqp", query_f, key_f) * score_scale
    fresh_score = jnp.einsum("rgqd,rgd->rgq", query_f, new_keys.astype(jnp.float32)) * score_scale
    is_valid = jnp.arange(span, dtype=jnp.int32)[None, :] < lengths[:, None]
    scores = jnp.where(is_valid[:, None, None, :], scores, -jnp.inf)
    every_score = jnp.concatenate([scores, fresh_score[:, :, :, None]], axis=3)
    weights = jax.nn.softmax(every_score, axis=3)
    every_value = jnp.concatenate([value_f, new_values.astype(jnp.float32)[:, :, None, :]], axis=2)
    output = jnp.einsum("rgqp,rgpd->rgqd", weights, every_value)
    return output.reshape(row_count, kv_heads * group_size * head_dim)


def expert_tables(route_ids, route_weight, expert_slot, capacity):
    row_count, top_count = route_ids.shape
    experts = expert_slot.shape[0]
    flat_ids = route_ids.reshape(row_count * top_count)
    onehot = (flat_ids[:, None] == jnp.arange(experts, dtype=jnp.int32)[None, :]).astype(jnp.int32)
    before = jnp.cumsum(onehot, axis=0) - onehot
    position = jnp.sum(before * onehot, axis=1)
    slot_ids = jnp.sum(onehot * expert_slot[None, :], axis=1)
    target = slot_ids * capacity + position
    placed = (target[:, None] == jnp.arange(experts * capacity, dtype=jnp.int32)[None, :]).astype(
        jnp.float32
    )
    placed = placed.reshape(row_count, top_count, experts * capacity)
    select = jnp.sum(placed, axis=1)
    weighted = jnp.sum(placed * route_weight[:, :, None], axis=1)
    return (
        select.T.reshape(experts, capacity, row_count),
        weighted.T.reshape(experts, capacity, row_count),
    )


def routed_device(
    queries,
    cache_keys,
    cache_values,
    new_keys,
    new_values,
    lengths,
    residual,
    norm_gain,
    routes,
    route_weights,
    expert_slot,
    gate_halves,
    up_halves,
    down_halves,
):
    own_rows = attend(queries, cache_keys, cache_values, new_keys, new_values, lengths)
    attention = lax.all_to_all(own_rows, "tp", split_axis=1, concat_axis=0, tiled=True)
    stream = (residual.astype(jnp.float32) + attention).astype(jnp.bfloat16)
    row_count = stream.shape[0]
    half_rows = row_count // 2
    top_count = routes.shape[1]
    experts = expert_slot.shape[0]
    tp_size = lax.axis_size("tp")
    ep_size = lax.axis_size("ep")
    tp_rank = lax.axis_index("tp")
    width_part = stream.shape[1]
    full_width = width_part * tp_size
    capacity = min(half_rows, 2 * half_rows * top_count // experts)
    gate_local = gate_halves[0]
    up_local = up_halves[0]
    down_local = down_halves[0]
    partials = []
    stream_f = stream.astype(jnp.float32)
    squares = lax.psum(jnp.sum(stream_f * stream_f, axis=1), "tp")
    gain_part = lax.dynamic_slice_in_dim(norm_gain, tp_rank * width_part, width_part).astype(
        jnp.float32
    )
    scaled = lax.rsqrt(squares / full_width + EPSILON)
    normed = (stream_f * scaled[:, None] * gain_part[None, :]).astype(jnp.bfloat16)
    gate_split = gate_local.reshape(tp_size, width_part, -1)
    up_split = up_local.reshape(tp_size, width_part, -1)
    down_split = down_local.reshape(-1, tp_size, width_part)
    for batch_index in range(2):
        row_start = batch_index * half_rows
        batch_rows = normed[row_start : row_start + half_rows]
        select, weighted = expert_tables(
            routes[row_start : row_start + half_rows],
            route_weights[row_start : row_start + half_rows],
            expert_slot,
            capacity,
        )
        select = jnp.repeat(select, 2, axis=0).transpose(1, 0, 2)
        weighted = jnp.repeat(weighted, 2, axis=0).transpose(1, 0, 2)
        outgoing = jnp.einsum(
            "cjr,rf->cjf",
            select.astype(jnp.bfloat16),
            batch_rows,
            preferred_element_type=jnp.float32,
        ).astype(jnp.bfloat16)
        arrived = lax.all_to_all(outgoing, ("ep", "tp"), split_axis=1, concat_axis=1, tiled=True)
        item_count = arrived.shape[0]
        blocks = arrived.reshape(item_count, ep_size, tp_size, width_part)
        gate_out = jnp.einsum(
            "cabf,bfh->cah", blocks, gate_split, preferred_element_type=jnp.float32
        )
        up_out = jnp.einsum("cabf,bfh->cah", blocks, up_split, preferred_element_type=jnp.float32)
        hidden = (jax.nn.silu(gate_out) * up_out).astype(jnp.bfloat16)
        result = jnp.einsum(
            "cah,hbf->cabf", hidden, down_split, preferred_element_type=jnp.float32
        ).astype(jnp.bfloat16)
        result = result.reshape(item_count, ep_size * tp_size, width_part)
        returned = lax.all_to_all(result, ("ep", "tp"), split_axis=1, concat_axis=1, tiled=True)
        partials.append(
            jnp.einsum(
                "cjr,cjf->rf",
                weighted,
                returned.astype(jnp.float32),
                precision=lax.Precision.HIGHEST,
            )
        )
    mixture = jnp.concatenate(partials, axis=0)
    return (stream.astype(jnp.float32) + mixture).astype(jnp.bfloat16)


def flip(value):
    return 1 - value


def layer_kernel(
    full_width,
    att_ref,
    residual_ref,
    gain_ref,
    table_ref,
    gate_ref,
    up_ref,
    down_ref,
    out_ref,
    att_in,
    stream_ref,
    sq_out,
    sq_in,
    rows_all,
    pieces,
    from_mate,
    from_b,
    from_a,
    from_z,
    wide_w,
    down_w,
    acc_ref,
    load_sem,
    att_send,
    att_recv,
    sq_send,
    sq_recv,
    go_send,
    z_recv,
    a_recv,
    b_recv,
    mate_recv,
    back_send,
    back_mate,
    back_b,
    back_a,
    back_z,
):
    ep = lax.axis_index("ep")
    tp = lax.axis_index("tp")
    z, y = ep // 2, ep % 2
    x, c = tp // 2, tp % 2
    hidden_width = gate_ref.shape[1]
    width = residual_ref.shape[1]
    own_rows = att_ref.shape[0]

    loads = [
        pltpu.make_async_copy(gate_ref, wide_w.at[:, pl.ds(0, hidden_width)], load_sem.at[0]),
        pltpu.make_async_copy(
            up_ref, wide_w.at[:, pl.ds(hidden_width, hidden_width)], load_sem.at[1]
        ),
        pltpu.make_async_copy(down_ref, down_w, load_sem.at[2]),
    ]
    for load in loads:
        load.start()

    z_of = [z, z + 1 - 2 * (z % 2), z + 2 - 4 * (z // 2), 3 - z]
    tp_of = [tp, tp + 1 - 2 * c, tp + 2 - 4 * x, 3 - tp]
    mate = (ep, tp_of[1])
    step_y = 1 - 2 * y
    step_x = 2 - 4 * x
    peer_a = (ep + (1 - c) * step_y, tp + c * step_x)
    peer_b = (ep + c * step_y, tp + (1 - c) * step_x)
    peer_z = [None] + [(2 * z_of[k] + y, tp) for k in (1, 2, 3)]
    own_a = y * (1 - c) + x * c
    own_b = x * (1 - c) + y * c

    def to(device):
        return {"ep": device[0], "tp": device[1]}

    barrier = pltpu.get_barrier_semaphore()
    greeted = [mate, peer_a, peer_b, (ep, tp_of[3])] + peer_z[1:]
    for device in greeted:
        pl.semaphore_signal(
            barrier, inc=1, device_id=to(device), device_id_type=pl.DeviceIdType.MESH
        )
    pl.semaphore_wait(barrier, len(greeted))

    sent = []

    def push(source, target, send_sem, recv_sem, device):
        copy = pltpu.make_async_remote_copy(
            src_ref=source,
            dst_ref=target,
            send_sem=send_sem,
            recv_sem=recv_sem,
            device_id=to(device),
            device_id_type=pl.DeviceIdType.MESH,
        )
        copy.start()
        sent.append(copy)

    def arrived(target, recv_sem, device):
        pltpu.make_async_remote_copy(
            src_ref=target,
            dst_ref=target,
            send_sem=recv_sem,
            recv_sem=recv_sem,
            device_id=to(device),
            device_id_type=pl.DeviceIdType.MESH,
        ).wait_recv()

    def columns(index):
        return pl.ds(pl.multiple_of(index * width, width), width)

    for d in (3, 2, 1):
        push(
            att_ref.at[:, columns(tp_of[d])],
            att_in.at[tp],
            att_send.at[d],
            att_recv.at[d],
            (ep, tp_of[d]),
        )
    att_in[tp] = att_ref[:, columns(tp)]
    for d in (1, 2, 3):
        arrived(att_in.at[tp_of[d]], att_recv.at[d], (ep, tp_of[d]))
    stream = (
        residual_ref[...].astype(jnp.float32) + att_in[...].reshape(4 * own_rows, width)
    ).astype(jnp.bfloat16)
    stream_ref[...] = stream
    stream_f = stream.astype(jnp.float32)
    row_count = stream.shape[0]
    own_sq = jnp.sum(stream_f * stream_f, axis=1, keepdims=True)
    sq_out[...] = jnp.broadcast_to(own_sq, (row_count, 128)).T[0:8, :]
    for d in (3, 2, 1):
        push(sq_out, sq_in.at[d - 1], sq_send.at[d], sq_recv.at[d], (ep, tp_of[d]))
    for d in (1, 2, 3):
        arrived(sq_in.at[d - 1], sq_recv.at[d], (ep, tp_of[d]))
    squares = sq_out[...] + sq_in[0] + sq_in[1] + sq_in[2]
    scaled = lax.rsqrt(squares / full_width + EPSILON)
    scaled = jnp.concatenate([scaled] * 16, axis=0).T[:, 0:1]
    normed = (stream_ref[...].astype(jnp.float32) * scaled * gain_ref[tp]).astype(jnp.bfloat16)
    rows_all[z, y, tp] = normed

    def place(ra, rb):
        a = own_a if ra == 0 else flip(own_a)
        b = own_b if rb == 0 else flip(own_b)
        return a * (1 - c) + b * c, a * c + b * (1 - c)

    def slot(k, ra, rb):
        y_at, x_at = place(ra, rb)
        return rows_all.at[z_of[k], y_at, 2 * x_at + c]

    def mate_slot(k, ra, rb):
        y_at, x_at = place(rb, ra)
        return rows_all.at[z_of[k], y_at, 2 * x_at + flip(c)]

    def go(block, index, recv_sem, device):
        push(block, block, go_send.at[index], recv_sem, device)

    def forward(k, ra, rb):
        block = slot(k, ra, rb)
        if (ra, rb) == (0, 0):
            go(block, k * 8, a_recv.at[k], peer_a)
            go(block, k * 8 + 1, b_recv.at[2 * k], peer_b)
        if (ra, rb) == (1, 0):
            go(block, k * 8 + 2, b_recv.at[2 * k + 1], peer_b)
        role = 2 * ra + rb
        go(block, k * 8 + 3 + role, mate_recv.at[4 * k + role], mate)

    def take_z(k):
        arrived(slot(k, 0, 0), z_recv.at[k], peer_z[k])
        forward(k, 0, 0)

    def take_a(k):
        arrived(slot(k, 1, 0), a_recv.at[k], peer_a)
        forward(k, 1, 0)

    def take_b(k, ra):
        arrived(slot(k, ra, 1), b_recv.at[2 * k + ra], peer_b)
        forward(k, ra, 1)

    slot_id = (ep * 4 + tp) // 2

    def compute(k):
        for ra in (0, 1):
            for rb in (0, 1):
                arrived(mate_slot(k, ra, rb), mate_recv.at[4 * k + 2 * ra + rb], mate)
        if k == 0:
            for load in loads:
                load.wait()
        z_at = z_of[k]
        rows = 2 * row_count

        acc_ref[...] = jnp.zeros_like(acc_ref)

        def add_part(t, carry):
            acc_ref[...] += jnp.dot(
                rows_all[z_at, :, t].reshape(rows, width),
                wide_w[columns(t), :],
                preferred_element_type=jnp.float32,
            )
            return carry

        lax.fori_loop(0, 4, add_part, 0)
        table = table_ref[z_at]
        lanes = lax.broadcasted_iota(jnp.int32, table.shape, 1)
        weight = jnp.sum(jnp.where(lanes == slot_id, table, 0.0), axis=1, keepdims=True)
        gate = acc_ref[:, 0:hidden_width]
        up = acc_ref[:, hidden_width : 2 * hidden_width]
        hidden = (gate / (1.0 + jnp.exp(-gate)) * up * weight).astype(jnp.bfloat16)
        for t in range(4):
            part = jnp.dot(
                hidden,
                down_w[:, t * width : (t + 1) * width],
                preferred_element_type=jnp.float32,
            ).astype(jnp.bfloat16)
            pieces[t % 2, z_at, :, t // 2] = part.reshape(2, row_count, width)
        push(pieces.at[flip(c), z_at], from_mate.at[z_at], back_send.at[8 * k], back_mate.at[k], mate)

    def back_1(k):
        z_at = z_of[k]
        arrived(from_mate.at[z_at], back_mate.at[k], mate)
        for rb in (1, 0):
            for ra in (1, 0):
                y_at, x_at = place(ra, rb)
                from_mate[z_at, y_at, x_at] = (
                    from_mate[z_at, y_at, x_at] + pieces[c, z_at, y_at, x_at]
                )
                if rb == 1:
                    push(
                        from_mate.at[z_at, y_at, x_at],
                        from_b.at[k, ra],
                        back_send.at[8 * k + 1 + ra],
                        back_b.at[2 * k + ra],
                        peer_b,
                    )

    def back_2(k):
        for ra in (1, 0):
            arrived(from_b.at[k, ra], back_b.at[2 * k + ra], peer_b)
            y_at, x_at = place(ra, 0)
            from_b[k, ra] = from_b[k, ra] + from_mate[z_of[k], y_at, x_at]
            if ra == 1:
                push(from_b.at[k, 1], from_a.at[k], back_send.at[8 * k + 3], back_a.at[k], peer_a)

    def back_3(k):
        arrived(from_a.at[k], back_a.at[k], peer_a)
        from_a[k] = from_a[k] + from_b[k, 0]
        if k > 0:
            push(from_a.at[k], from_z.at[k - 1], back_send.at[8 * k + 4], back_z.at[k], peer_z[k])

    for k in (1, 2, 3):
        push(slot(0, 0, 0), slot(0, 0, 0), go_send.at[32 + k], z_recv.at[k], peer_z[k])
    forward(0, 0, 0)
    take_z(1)
    take_a(0)
    take_b(0, 0)
    take_z(2)
    take_a(1)
    take_b(0, 1)
    take_b(1, 0)
    compute(0)
    take_z(3)
    take_a(2)
    take_b(1, 1)
    take_b(2, 0)
    compute(1)
    back_1(0)
    take_a(3)
    take_b(2, 1)
    take_b(3, 0)
    compute(2)
    back_1(1)
    back_2(0)
    take_b(3, 1)
    compute(3)
    back_1(2)
    back_2(1)
    back_3(0)
    back_1(3)
    back_2(2)
    back_3(1)
    back_2(3)
    back_3(2)
    back_3(3)
    total = stream_ref[...].astype(jnp.float32) + from_a[0].astype(jnp.float32)
    for k in (1, 2, 3):
        arrived(from_z.at[k - 1], back_z.at[k], peer_z[k])
        total = total + from_z[k - 1].astype(jnp.float32)
    out_ref[...] = total.astype(jnp.bfloat16)
    for copy in sent:
        copy.wait_send()


def dense_device(
    queries,
    cache_keys,
    cache_values,
    new_keys,
    new_values,
    lengths,
    residual,
    norm_gain,
    routes,
    route_weights,
    expert_slot,
    gate_halves,
    up_halves,
    down_halves,
):
    experts = expert_slot.shape[0]
    row_count, width = residual.shape
    hidden_width = gate_halves.shape[2]
    full_width = norm_gain.shape[0]
    chosen = routes[:, :, None] == jnp.arange(experts, dtype=jnp.int32)
    by_expert = jnp.sum(jnp.where(chosen, route_weights[:, :, None], 0.0), axis=1)
    slots = expert_slot[:, None] == jnp.arange(experts, dtype=jnp.int32)[None, :]
    table = jnp.sum(jnp.where(slots[None], by_expert[:, :, None], 0.0), axis=1)
    table = lax.all_gather(table, "ep", axis=0, tiled=True).reshape(4, 2 * row_count, experts)
    own_rows = attend(queries, cache_keys, cache_values, new_keys, new_values, lengths)
    block = (row_count, width)
    vmem = pl.BlockSpec(memory_space=pltpu.VMEM)
    anywhere = pl.BlockSpec(memory_space=pl.ANY)
    dma = pltpu.SemaphoreType.DMA
    return pl.pallas_call(
        functools.partial(layer_kernel, full_width),
        out_shape=jax.ShapeDtypeStruct(block, jnp.bfloat16),
        in_specs=[vmem] * 4 + [anywhere] * 3,
        out_specs=vmem,
        scratch_shapes=[
            pltpu.VMEM((4, row_count // 4, width), jnp.float32),
            pltpu.VMEM(block, jnp.bfloat16),
            pltpu.VMEM((8, 128), jnp.float32),
            pltpu.VMEM((3, 8, 128), jnp.float32),
            pltpu.VMEM((4, 2, 4) + block, jnp.bfloat16),
            pltpu.VMEM((2, 4, 2, 2) + block, jnp.bfloat16),
            pltpu.VMEM((4, 2, 2) + block, jnp.bfloat16),
            pltpu.VMEM((4, 2) + block, jnp.bfloat16),
            pltpu.VMEM((4,) + block, jnp.bfloat16),
            pltpu.VMEM((3,) + block, jnp.bfloat16),
            pltpu.VMEM((full_width, 2 * hidden_width), jnp.bfloat16),
            pltpu.VMEM((hidden_width, full_width), jnp.bfloat16),
            pltpu.VMEM((2 * row_count, 2 * hidden_width), jnp.float32),
            dma((3,)),
            dma((4,)),
            dma((4,)),
            dma((4,)),
            dma((4,)),
            dma((36,)),
            dma((4,)),
            dma((4,)),
            dma((8,)),
            dma((16,)),
            dma((32,)),
            dma((4,)),
            dma((8,)),
            dma((4,)),
            dma((4,)),
        ],
        compiler_params=pltpu.CompilerParams(
            collective_id=0, has_side_effects=True, vmem_limit_bytes=58 * 1024 * 1024
        ),
    )(
        own_rows,
        residual,
        norm_gain.astype(jnp.float32).reshape(4, 1, width),
        table,
        gate_halves[0],
        up_halves[0],
        down_halves[0],
    )


def on_device(*args):
    routes, expert_slot = args[8], args[10]
    half_rows = routes.shape[0] // 2
    capacity = min(half_rows, 2 * half_rows * routes.shape[1] // expert_slot.shape[0])
    grid = (lax.axis_size("ep"), lax.axis_size("tp"))
    if capacity == half_rows and grid == (8, 4) and routes.shape[0] == 128:
        return dense_device(*args)
    return routed_device(*args)


def solution(mesh):
    return jax.shard_map(
        on_device,
        mesh=mesh,
        in_specs=(
            P(("groups", "ep", "tp"), None),
            P(("groups", "ep", "tp"), None, None, None),
            P(("groups", "ep", "tp"), None, None, None),
            P(("groups", "ep", "tp"), None, None),
            P(("groups", "ep", "tp"), None, None),
            P(("groups", "ep", "tp")),
            P(("groups", "ep"), "tp"),
            P(),
            P(("groups", "ep"), None),
            P(("groups", "ep"), None),
            P(),
            P(("ep", "tp"), None, None),
            P(("ep", "tp"), None, None),
            P(("ep", "tp"), None, None),
        ),
        out_specs=P(("groups", "ep"), "tp"),
        check_vma=False,
    )
```

```python
import functools

import jax
import jax.numpy as jnp
from jax import lax
from jax.experimental import pallas as pl
from jax.experimental.pallas import tpu as pltpu
from jax.sharding import PartitionSpec as P

EPSILON = 1e-06
UNROLL = 4


def attend(queries, cache_keys, cache_values, new_keys, new_values, lengths):
    row_count = queries.shape[0]
    kv_heads = new_keys.shape[1]
    head_dim = new_keys.shape[2]
    group_size = queries.shape[1] // (kv_heads * head_dim)
    span = cache_keys.shape[2] * 2
    query_f = queries.reshape(row_count, kv_heads, group_size, head_dim).astype(jnp.float32)
    key_f = cache_keys.reshape(row_count, kv_heads, span, head_dim).astype(jnp.float32)
    value_f = cache_values.reshape(row_count, kv_heads, span, head_dim).astype(jnp.float32)
    score_scale = 1.0 / jnp.sqrt(jnp.float32(head_dim))
    scores = jnp.einsum("rgqd,rgpd->rgqp", query_f, key_f) * score_scale
    fresh_score = jnp.einsum("rgqd,rgd->rgq", query_f, new_keys.astype(jnp.float32)) * score_scale
    is_valid = jnp.arange(span, dtype=jnp.int32)[None, :] < lengths[:, None]
    scores = jnp.where(is_valid[:, None, None, :], scores, -jnp.inf)
    every_score = jnp.concatenate([scores, fresh_score[:, :, :, None]], axis=3)
    weights = jax.nn.softmax(every_score, axis=3)
    every_value = jnp.concatenate([value_f, new_values.astype(jnp.float32)[:, :, None, :]], axis=2)
    output = jnp.einsum("rgqp,rgpd->rgqd", weights, every_value)
    return output.reshape(row_count, kv_heads * group_size * head_dim)


def expert_tables(route_ids, route_weight, expert_slot, capacity):
    row_count, top_count = route_ids.shape
    experts = expert_slot.shape[0]
    flat_ids = route_ids.reshape(row_count * top_count)
    onehot = (flat_ids[:, None] == jnp.arange(experts, dtype=jnp.int32)[None, :]).astype(jnp.int32)
    before = jnp.cumsum(onehot, axis=0) - onehot
    position = jnp.sum(before * onehot, axis=1)
    slot_ids = jnp.sum(onehot * expert_slot[None, :], axis=1)
    target = slot_ids * capacity + position
    placed = (target[:, None] == jnp.arange(experts * capacity, dtype=jnp.int32)[None, :]).astype(
        jnp.float32
    )
    placed = placed.reshape(row_count, top_count, experts * capacity)
    select = jnp.sum(placed, axis=1)
    weighted = jnp.sum(placed * route_weight[:, :, None], axis=1)
    return (
        select.T.reshape(experts, capacity, row_count),
        weighted.T.reshape(experts, capacity, row_count),
    )


def routed_device(
    queries,
    cache_keys,
    cache_values,
    new_keys,
    new_values,
    lengths,
    residual,
    norm_gain,
    routes,
    route_weights,
    expert_slot,
    gate_halves,
    up_halves,
    down_halves,
):
    own_rows = attend(queries, cache_keys, cache_values, new_keys, new_values, lengths)
    attention = lax.all_to_all(own_rows, "tp", split_axis=1, concat_axis=0, tiled=True)
    stream = (residual.astype(jnp.float32) + attention).astype(jnp.bfloat16)
    row_count = stream.shape[0]
    half_rows = row_count // 2
    top_count = routes.shape[1]
    experts = expert_slot.shape[0]
    tp_size = lax.axis_size("tp")
    ep_size = lax.axis_size("ep")
    tp_rank = lax.axis_index("tp")
    width_part = stream.shape[1]
    full_width = width_part * tp_size
    capacity = min(half_rows, 2 * half_rows * top_count // experts)
    gate_local = gate_halves[0]
    up_local = up_halves[0]
    down_local = down_halves[0]
    partials = []
    stream_f = stream.astype(jnp.float32)
    squares = lax.psum(jnp.sum(stream_f * stream_f, axis=1), "tp")
    gain_part = lax.dynamic_slice_in_dim(norm_gain, tp_rank * width_part, width_part).astype(
        jnp.float32
    )
    scaled = lax.rsqrt(squares / full_width + EPSILON)
    normed = (stream_f * scaled[:, None] * gain_part[None, :]).astype(jnp.bfloat16)
    gate_split = gate_local.reshape(tp_size, width_part, -1)
    up_split = up_local.reshape(tp_size, width_part, -1)
    down_split = down_local.reshape(-1, tp_size, width_part)
    for batch_index in range(2):
        row_start = batch_index * half_rows
        batch_rows = normed[row_start : row_start + half_rows]
        select, weighted = expert_tables(
            routes[row_start : row_start + half_rows],
            route_weights[row_start : row_start + half_rows],
            expert_slot,
            capacity,
        )
        select = jnp.repeat(select, 2, axis=0).transpose(1, 0, 2)
        weighted = jnp.repeat(weighted, 2, axis=0).transpose(1, 0, 2)
        outgoing = jnp.einsum(
            "cjr,rf->cjf",
            select.astype(jnp.bfloat16),
            batch_rows,
            preferred_element_type=jnp.float32,
        ).astype(jnp.bfloat16)
        arrived = lax.all_to_all(outgoing, ("ep", "tp"), split_axis=1, concat_axis=1, tiled=True)
        item_count = arrived.shape[0]
        blocks = arrived.reshape(item_count, ep_size, tp_size, width_part)
        gate_out = jnp.einsum(
            "cabf,bfh->cah", blocks, gate_split, preferred_element_type=jnp.float32
        )
        up_out = jnp.einsum("cabf,bfh->cah", blocks, up_split, preferred_element_type=jnp.float32)
        hidden = (jax.nn.silu(gate_out) * up_out).astype(jnp.bfloat16)
        result = jnp.einsum(
            "cah,hbf->cabf", hidden, down_split, preferred_element_type=jnp.float32
        ).astype(jnp.bfloat16)
        result = result.reshape(item_count, ep_size * tp_size, width_part)
        returned = lax.all_to_all(result, ("ep", "tp"), split_axis=1, concat_axis=1, tiled=True)
        partials.append(
            jnp.einsum(
                "cjr,cjf->rf",
                weighted,
                returned.astype(jnp.float32),
                precision=lax.Precision.HIGHEST,
            )
        )
    mixture = jnp.concatenate(partials, axis=0)
    return (stream.astype(jnp.float32) + mixture).astype(jnp.bfloat16)


def flip(value):
    return 1 - value


def layer_kernel(
    full_width,
    lengths_ref,
    query_ref,
    key_ref,
    value_ref,
    fresh_key_ref,
    fresh_value_ref,
    residual_ref,
    gain_ref,
    table_ref,
    gate_ref,
    up_ref,
    down_ref,
    out_ref,
    keys,
    values,
    heads_out,
    att_out,
    att_in,
    stream_ref,
    sq_out,
    sq_in,
    tables,
    rows_all,
    pieces,
    from_mate,
    from_b,
    from_a,
    from_z,
    wide_w,
    down_w,
    acc_ref,
    load_sem,
    att_send,
    att_recv,
    sq_send,
    sq_recv,
    table_send,
    table_z,
    table_y,
    go_send,
    z_recv,
    a_recv,
    b_recv,
    mate_recv,
    back_send,
    back_mate,
    back_b,
    back_a,
    back_z,
):
    ep = lax.axis_index("ep")
    tp = lax.axis_index("tp")
    z, y = ep // 2, ep % 2
    x, c = tp // 2, tp % 2
    hidden_width = gate_ref.shape[1]
    row_count, width = residual_ref.shape
    half_rows = row_count // 2
    own_rows, head_count, head_dim = query_ref.shape
    own_half = own_rows // 2
    kv_heads = fresh_key_ref.shape[1]
    span = key_ref.shape[1] // kv_heads
    group = head_count // kv_heads

    def half_load(source, target, h, index):
        part = pl.ds(h * own_half, own_half)
        return pltpu.make_async_copy(source.at[part], target.at[part], load_sem.at[index])

    cache_loads = [
        [half_load(key_ref, keys, h, 2 * h), half_load(value_ref, values, h, 2 * h + 1)]
        for h in (0, 1)
    ]
    loads = [
        pltpu.make_async_copy(gate_ref, wide_w.at[:, pl.ds(0, hidden_width)], load_sem.at[4]),
        pltpu.make_async_copy(
            up_ref, wide_w.at[:, pl.ds(hidden_width, hidden_width)], load_sem.at[5]
        ),
        pltpu.make_async_copy(down_ref, down_w, load_sem.at[6]),
    ]
    for load in cache_loads[0] + cache_loads[1] + loads:
        load.start()

    z_of = [z, z + 1 - 2 * (z % 2), z + 2 - 4 * (z // 2), 3 - z]
    tp_of = [tp, tp + 1 - 2 * c, tp + 2 - 4 * x, 3 - tp]
    mate = (ep, tp_of[1])
    step_y = 1 - 2 * y
    step_x = 2 - 4 * x
    peer_y = (ep + step_y, tp)
    peer_a = (ep + (1 - c) * step_y, tp + c * step_x)
    peer_b = (ep + c * step_y, tp + (1 - c) * step_x)
    peer_z = [None] + [(2 * z_of[k] + y, tp) for k in (1, 2, 3)]
    own_a = y * (1 - c) + x * c
    own_b = x * (1 - c) + y * c

    def to(device):
        return {"ep": device[0], "tp": device[1]}

    barrier = pltpu.get_barrier_semaphore()
    greeted = [mate, peer_a, peer_b, (ep, tp_of[3])] + peer_z[1:]
    for device in greeted:
        pl.semaphore_signal(
            barrier, inc=1, device_id=to(device), device_id_type=pl.DeviceIdType.MESH
        )

    sent = []

    def push(source, target, send_sem, recv_sem, device):
        copy = pltpu.make_async_remote_copy(
            src_ref=source,
            dst_ref=target,
            send_sem=send_sem,
            recv_sem=recv_sem,
            device_id=to(device),
            device_id_type=pl.DeviceIdType.MESH,
        )
        copy.start()
        sent.append(copy)

    def arrived(target, recv_sem, device):
        pltpu.make_async_remote_copy(
            src_ref=target,
            dst_ref=target,
            send_sem=recv_sem,
            recv_sem=recv_sem,
            device_id=to(device),
            device_id_type=pl.DeviceIdType.MESH,
        ).wait_recv()

    def columns(index):
        return pl.ds(pl.multiple_of(index * width, width), width)

    score_scale = 1.0 / float(head_dim) ** 0.5
    head_at = lax.broadcasted_iota(jnp.int32, (head_count, kv_heads * span), 0)
    key_at = lax.broadcasted_iota(jnp.int32, (head_count, kv_heads * span), 1)
    same_group = head_at // group == key_at // span
    position = jnp.where(same_group, key_at % span, span)

    def per_head(value):
        return jnp.concatenate(
            [jnp.broadcast_to(value[g : g + 1], (group, head_dim)) for g in range(kv_heads)], axis=0
        )

    def attend_row(row, at):
        query = query_ref[row]
        scores = lax.dot_general(
            query, keys[row], (((1,), (1,)), ((), ())), preferred_element_type=jnp.float32
        )
        scores = jnp.where(position < lengths_ref[row], scores * score_scale, -1e30)
        fresh_key = per_head(fresh_key_ref[row].astype(jnp.float32))
        fresh = (
            jnp.sum(query.astype(jnp.float32) * fresh_key, axis=1, keepdims=True) * score_scale
        )
        top = jnp.maximum(jnp.max(scores, axis=1, keepdims=True), fresh)
        weights = jnp.exp(scores - top)
        fresh_weight = jnp.exp(fresh - top)
        total = jnp.sum(weights, axis=1, keepdims=True) + fresh_weight
        mixed = jnp.dot(
            weights.astype(jnp.bfloat16), values[row], preferred_element_type=jnp.float32
        )
        mixed = mixed + fresh_weight * per_head(fresh_value_ref[row].astype(jnp.float32))
        heads_out[at] = mixed / total

    def attend_half(h):
        for load in cache_loads[h]:
            load.wait()

        def some_rows(i, carry):
            for u in range(UNROLL):
                attend_row(h * own_half + i * UNROLL + u, i * UNROLL + u)
            return carry

        lax.fori_loop(0, own_half // UNROLL, some_rows, 0)
        per_part = head_count // 4
        for t in range(4):
            part = heads_out[:, t * per_part : (t + 1) * per_part, :]
            att_out[h, t] = part.reshape(own_half, width).astype(jnp.bfloat16)

    def send_attention(h):
        for d in (3, 2, 1):
            push(
                att_out.at[h, tp_of[d]],
                att_in.at[h, tp],
                att_send.at[4 * h + d],
                att_recv.at[4 * h + d],
                (ep, tp_of[d]),
            )
        att_in[h, tp] = att_out[h, tp]

    def own_squares(h):
        for d in (1, 2, 3):
            arrived(att_in.at[h, tp_of[d]], att_recv.at[4 * h + d], (ep, tp_of[d]))
        residual = jnp.concatenate(
            [
                residual_ref[(2 * t + h) * own_half : (2 * t + h + 1) * own_half]
                for t in range(4)
            ],
            axis=0,
        )
        attention = att_in[h].reshape(half_rows, width)
        stream = (residual.astype(jnp.float32) + attention.astype(jnp.float32)).astype(
            jnp.bfloat16
        )
        stream_ref[h] = stream
        stream_f = stream.astype(jnp.float32)
        rows_all[z, y, tp, h * half_rows : (h + 1) * half_rows] = (
            stream_f * gain_ref[tp]
        ).astype(jnp.bfloat16)
        return jnp.sum(stream_f * stream_f, axis=1, keepdims=True)

    def push_table(k):
        push(
            tables.at[z_of[k], y],
            tables.at[z_of[k], y],
            table_send.at[4 + k],
            table_y.at[k],
            peer_y,
        )

    def place(ra, rb):
        a = own_a if ra == 0 else flip(own_a)
        b = own_b if rb == 0 else flip(own_b)
        return a * (1 - c) + b * c, a * c + b * (1 - c)

    def slot(n, ra, rb):
        y_at, x_at = place(ra, rb)
        return rows_all.at[
            z_of[n // 2], y_at, 2 * x_at + c, pl.ds(n % 2 * half_rows, half_rows)
        ]

    def mate_slot(n, ra, rb):
        y_at, x_at = place(rb, ra)
        return rows_all.at[
            z_of[n // 2], y_at, 2 * x_at + flip(c), pl.ds(n % 2 * half_rows, half_rows)
        ]

    def go(block, index, recv_sem, device):
        push(block, block, go_send.at[index], recv_sem, device)

    def forward(n, ra, rb):
        block = slot(n, ra, rb)
        if (ra, rb) == (0, 0):
            go(block, n * 8, a_recv.at[n], peer_a)
            go(block, n * 8 + 1, b_recv.at[2 * n], peer_b)
        if (ra, rb) == (1, 0):
            go(block, n * 8 + 2, b_recv.at[2 * n + 1], peer_b)
        role = 2 * ra + rb
        go(block, n * 8 + 3 + role, mate_recv.at[4 * n + role], mate)

    def begin(h):
        for k in (1, 2, 3):
            go(slot(h, 0, 0), 64 + 3 * h + k - 1, z_recv.at[2 * k + h], peer_z[k])
        forward(h, 0, 0)

    def take_z(n):
        if n >= 2:
            arrived(slot(n, 0, 0), z_recv.at[n], peer_z[n // 2])
            forward(n, 0, 0)

    def take_a(n):
        arrived(slot(n, 1, 0), a_recv.at[n], peer_a)
        forward(n, 1, 0)

    def take_b(n, ra):
        arrived(slot(n, ra, 1), b_recv.at[2 * n + ra], peer_b)
        forward(n, ra, 1)

    slot_id = (ep * 4 + tp) // 2

    def compute(n):
        k, h = n // 2, n % 2
        z_at = z_of[k]
        for ra in (0, 1):
            for rb in (0, 1):
                arrived(mate_slot(n, ra, rb), mate_recv.at[4 * n + 2 * ra + rb], mate)
        if n == 0:
            for load in loads:
                load.wait()
        if h == 0:
            arrived(tables.at[z_at, flip(y)], table_y.at[k], peer_y)
        span_rows = pl.ds(h * half_rows, half_rows)
        acc_ref[...] = jnp.zeros_like(acc_ref)

        def add_part(t, carry):
            acc_ref[...] += jnp.dot(
                rows_all[z_at, :, t, span_rows].reshape(row_count, width),
                wide_w[columns(t), :],
                preferred_element_type=jnp.float32,
            )
            return carry

        lax.fori_loop(0, 4, add_part, 0)
        weights = []
        scales = []
        for y_at in (0, 1):
            table = tables[z_at, y_at]
            lines = lax.broadcasted_iota(jnp.int32, table.shape, 0)
            line = jnp.sum(jnp.where(lines == slot_id, table, 0.0), axis=0, keepdims=True)
            weights.append(
                jnp.broadcast_to(line, (row_count, row_count)).T[
                    h * half_rows : (h + 1) * half_rows, 0:1
                ]
            )
            line = table[table.shape[0] - 8 : table.shape[0] - 7]
            scales.append(
                jnp.broadcast_to(line, (row_count, row_count)).T[
                    h * half_rows : (h + 1) * half_rows, 0:1
                ]
            )
        weight = jnp.concatenate(weights, axis=0)
        scale = jnp.concatenate(scales, axis=0)
        gate = acc_ref[:, 0:hidden_width] * scale
        up = acc_ref[:, hidden_width : 2 * hidden_width] * scale
        hidden = (gate / (1.0 + jnp.exp(-gate)) * up * weight).astype(jnp.bfloat16)
        for t in range(4):
            part = jnp.dot(
                hidden,
                down_w[:, t * width : (t + 1) * width],
                preferred_element_type=jnp.float32,
            ).astype(jnp.bfloat16)
            pieces[h, t % 2, z_at, :, t // 2] = part.reshape(2, half_rows, width)
        push(
            pieces.at[h, flip(c), z_at],
            from_mate.at[h, z_at],
            back_send.at[8 * n],
            back_mate.at[n],
            mate,
        )

    def back_1(n):
        h, z_at = n % 2, z_of[n // 2]
        arrived(from_mate.at[h, z_at], back_mate.at[n], mate)
        for rb in (1, 0):
            for ra in (1, 0):
                y_at, x_at = place(ra, rb)
                from_mate[h, z_at, y_at, x_at] = (
                    from_mate[h, z_at, y_at, x_at] + pieces[h, c, z_at, y_at, x_at]
                )
                if rb == 1:
                    push(
                        from_mate.at[h, z_at, y_at, x_at],
                        from_b.at[n, ra],
                        back_send.at[8 * n + 1 + ra],
                        back_b.at[2 * n + ra],
                        peer_b,
                    )

    def back_2(n):
        for ra in (1, 0):
            arrived(from_b.at[n, ra], back_b.at[2 * n + ra], peer_b)
            y_at, x_at = place(ra, 0)
            from_b[n, ra] = from_b[n, ra] + from_mate[n % 2, z_of[n // 2], y_at, x_at]
            if ra == 1:
                push(from_b.at[n, 1], from_a.at[n], back_send.at[8 * n + 3], back_a.at[n], peer_a)

    def back_3(n):
        arrived(from_a.at[n], back_a.at[n], peer_a)
        from_a[n] = from_a[n] + from_b[n, 0]
        if n >= 2:
            push(
                from_a.at[n], from_z.at[n], back_send.at[8 * n + 4], back_z.at[n], peer_z[n // 2]
            )

    def finish(h):
        total = stream_ref[h].astype(jnp.float32) + from_a[h].astype(jnp.float32)
        for k in (1, 2, 3):
            n = 2 * k + h
            arrived(from_z.at[n], back_z.at[n], peer_z[k])
            total = total + from_z[n].astype(jnp.float32)
        total = total.astype(jnp.bfloat16)
        for t in range(4):
            out_ref[(2 * t + h) * own_half : (2 * t + h + 1) * own_half] = total[
                t * own_half : (t + 1) * own_half
            ]

    attend_half(0)
    pl.semaphore_wait(barrier, len(greeted))
    send_attention(0)
    attend_half(1)
    send_attention(1)
    squares_0 = own_squares(0)
    begin(0)
    squares_1 = own_squares(1)
    begin(1)
    own_sq = jnp.concatenate([squares_0, squares_1], axis=0)
    sq_out[...] = jnp.broadcast_to(own_sq, (row_count, row_count)).T[0:8, :]
    for d in (3, 2, 1):
        push(sq_out, sq_in.at[d - 1], sq_send.at[d], sq_recv.at[d], (ep, tp_of[d]))

    def spread_tables():
        for d in (1, 2, 3):
            arrived(sq_in.at[d - 1], sq_recv.at[d], (ep, tp_of[d]))
        squares = sq_out[...] + sq_in[0] + sq_in[1] + sq_in[2]
        scaled = lax.rsqrt(squares / full_width + EPSILON)
        tables[z, y] = jnp.concatenate([table_ref[...], scaled], axis=0)
        for k in (1, 2, 3):
            push(tables.at[z, y], tables.at[z, y], table_send.at[k], table_z.at[k], peer_z[k])
        push_table(0)

    def relay_tables():
        for k in (1, 2, 3):
            arrived(tables.at[z_of[k], y], table_z.at[k], peer_z[k])
            push_table(k)

    order = (0, 1, 2, 4, 6, 3, 5, 7)

    def staged(action, step, lag, *more):
        if 0 <= step - lag < len(order):
            action(order[step - lag], *more)

    for step in range(1, len(order) + 6):
        if step == 2:
            spread_tables()
        if step == 4:
            relay_tables()
        staged(take_z, step, 0)
        staged(take_a, step, 1)
        staged(take_b, step, 1, 0)
        staged(take_b, step, 2, 1)
        staged(back_1, step, 4)
        staged(back_2, step, 5)
        staged(back_3, step, 6)
        staged(compute, step, 3)
    for h in (0, 1):
        finish(h)
    for copy in sent:
        copy.wait_send()


def dense_device(
    queries,
    cache_keys,
    cache_values,
    new_keys,
    new_values,
    lengths,
    residual,
    norm_gain,
    routes,
    route_weights,
    expert_slot,
    gate_halves,
    up_halves,
    down_halves,
):
    experts = expert_slot.shape[0]
    row_count, width = residual.shape
    half_rows = row_count // 2
    hidden_width = gate_halves.shape[2]
    full_width = norm_gain.shape[0]
    own_rows, kv_heads, head_dim = new_keys.shape
    head_count = queries.shape[1] // head_dim
    keys_per_row = cache_keys.shape[1] * cache_keys.shape[2]
    chosen = routes[:, :, None] == jnp.arange(experts, dtype=jnp.int32)
    by_expert = jnp.sum(jnp.where(chosen, route_weights[:, :, None], 0.0), axis=1)
    slots = expert_slot[:, None] == jnp.arange(experts, dtype=jnp.int32)[None, :]
    table = jnp.sum(jnp.where(slots[None], by_expert[:, :, None], 0.0), axis=1)
    table = table.reshape(4, 2, own_rows // 2, experts).transpose(3, 1, 0, 2)
    table = table.reshape(experts, row_count)
    block = (row_count, width)
    half = (half_rows, width)
    cache = (own_rows, keys_per_row, head_dim)
    vmem = pl.BlockSpec(memory_space=pltpu.VMEM)
    smem = pl.BlockSpec(memory_space=pltpu.SMEM)
    anywhere = pl.BlockSpec(memory_space=pl.ANY)
    dma = pltpu.SemaphoreType.DMA
    return pl.pallas_call(
        functools.partial(layer_kernel, full_width),
        out_shape=jax.ShapeDtypeStruct(block, jnp.bfloat16),
        in_specs=[smem, vmem, anywhere, anywhere] + [vmem] * 5 + [anywhere] * 3,
        out_specs=vmem,
        scratch_shapes=[
            pltpu.VMEM(cache, jnp.bfloat16),
            pltpu.VMEM(cache, jnp.bfloat16),
            pltpu.VMEM((own_rows // 2, head_count, head_dim), jnp.float32),
            pltpu.VMEM((2, 4, own_rows // 2, width), jnp.bfloat16),
            pltpu.VMEM((2, 4, own_rows // 2, width), jnp.bfloat16),
            pltpu.VMEM((2,) + half, jnp.bfloat16),
            pltpu.VMEM((8, row_count), jnp.float32),
            pltpu.VMEM((3, 8, row_count), jnp.float32),
            pltpu.VMEM((4, 2, experts + 8, row_count), jnp.float32),
            pltpu.VMEM((4, 2, 4) + block, jnp.bfloat16),
            pltpu.VMEM((2, 2, 4, 2, 2) + half, jnp.bfloat16),
            pltpu.VMEM((2, 4, 2, 2) + half, jnp.bfloat16),
            pltpu.VMEM((8, 2) + half, jnp.bfloat16),
            pltpu.VMEM((8,) + half, jnp.bfloat16),
            pltpu.VMEM((8,) + half, jnp.bfloat16),
            pltpu.VMEM((full_width, 2 * hidden_width), jnp.bfloat16),
            pltpu.VMEM((hidden_width, full_width), jnp.bfloat16),
            pltpu.VMEM((row_count, 2 * hidden_width), jnp.float32),
            dma((7,)),
            dma((8,)),
            dma((8,)),
            dma((4,)),
            dma((4,)),
            dma((8,)),
            dma((4,)),
            dma((4,)),
            dma((72,)),
            dma((8,)),
            dma((8,)),
            dma((16,)),
            dma((32,)),
            dma((64,)),
            dma((8,)),
            dma((16,)),
            dma((8,)),
            dma((8,)),
        ],
        compiler_params=pltpu.CompilerParams(
            collective_id=0, has_side_effects=True, vmem_limit_bytes=58 * 1024 * 1024
        ),
    )(
        lengths,
        queries.reshape(own_rows, head_count, head_dim),
        cache_keys.reshape(cache),
        cache_values.reshape(cache),
        new_keys,
        new_values,
        residual,
        norm_gain.astype(jnp.float32).reshape(4, 1, width),
        table,
        gate_halves[0],
        up_halves[0],
        down_halves[0],
    )


def on_device(*args):
    routes, expert_slot = args[8], args[10]
    half_rows = routes.shape[0] // 2
    capacity = min(half_rows, 2 * half_rows * routes.shape[1] // expert_slot.shape[0])
    grid = (lax.axis_size("ep"), lax.axis_size("tp"))
    if capacity == half_rows and grid == (8, 4) and routes.shape[0] == 128:
        return dense_device(*args)
    return routed_device(*args)


def solution(mesh):
    return jax.shard_map(
        on_device,
        mesh=mesh,
        in_specs=(
            P(("groups", "ep", "tp"), None),
            P(("groups", "ep", "tp"), None, None, None),
            P(("groups", "ep", "tp"), None, None, None),
            P(("groups", "ep", "tp"), None, None),
            P(("groups", "ep", "tp"), None, None),
            P(("groups", "ep", "tp")),
            P(("groups", "ep"), "tp"),
            P(),
            P(("groups", "ep"), None),
            P(("groups", "ep"), None),
            P(),
            P(("ep", "tp"), None, None),
            P(("ep", "tp"), None, None),
            P(("ep", "tp"), None, None),
        ),
        out_specs=P(("groups", "ep"), "tp"),
        check_vma=False,
    )
```

```python
import functools

import jax
import jax.numpy as jnp
from jax import lax
from jax.experimental import pallas as pl
from jax.experimental.pallas import tpu as pltpu
from jax.sharding import PartitionSpec as P

EPSILON = 1e-06
UNROLL = 8


def attend(queries, cache_keys, cache_values, new_keys, new_values, lengths):
    row_count = queries.shape[0]
    kv_heads = new_keys.shape[1]
    head_dim = new_keys.shape[2]
    group_size = queries.shape[1] // (kv_heads * head_dim)
    span = cache_keys.shape[2] * 2
    query_f = queries.reshape(row_count, kv_heads, group_size, head_dim).astype(jnp.float32)
    key_f = cache_keys.reshape(row_count, kv_heads, span, head_dim).astype(jnp.float32)
    value_f = cache_values.reshape(row_count, kv_heads, span, head_dim).astype(jnp.float32)
    score_scale = 1.0 / jnp.sqrt(jnp.float32(head_dim))
    scores = jnp.einsum("rgqd,rgpd->rgqp", query_f, key_f) * score_scale
    fresh_score = jnp.einsum("rgqd,rgd->rgq", query_f, new_keys.astype(jnp.float32)) * score_scale
    is_valid = jnp.arange(span, dtype=jnp.int32)[None, :] < lengths[:, None]
    scores = jnp.where(is_valid[:, None, None, :], scores, -jnp.inf)
    every_score = jnp.concatenate([scores, fresh_score[:, :, :, None]], axis=3)
    weights = jax.nn.softmax(every_score, axis=3)
    every_value = jnp.concatenate([value_f, new_values.astype(jnp.float32)[:, :, None, :]], axis=2)
    output = jnp.einsum("rgqp,rgpd->rgqd", weights, every_value)
    return output.reshape(row_count, kv_heads * group_size * head_dim)


def expert_tables(route_ids, route_weight, expert_slot, capacity):
    row_count, top_count = route_ids.shape
    experts = expert_slot.shape[0]
    flat_ids = route_ids.reshape(row_count * top_count)
    onehot = (flat_ids[:, None] == jnp.arange(experts, dtype=jnp.int32)[None, :]).astype(jnp.int32)
    before = jnp.cumsum(onehot, axis=0) - onehot
    position = jnp.sum(before * onehot, axis=1)
    slot_ids = jnp.sum(onehot * expert_slot[None, :], axis=1)
    target = slot_ids * capacity + position
    placed = (target[:, None] == jnp.arange(experts * capacity, dtype=jnp.int32)[None, :]).astype(
        jnp.float32
    )
    placed = placed.reshape(row_count, top_count, experts * capacity)
    select = jnp.sum(placed, axis=1)
    weighted = jnp.sum(placed * route_weight[:, :, None], axis=1)
    return (
        select.T.reshape(experts, capacity, row_count),
        weighted.T.reshape(experts, capacity, row_count),
    )


def routed_device(
    queries,
    cache_keys,
    cache_values,
    new_keys,
    new_values,
    lengths,
    residual,
    norm_gain,
    routes,
    route_weights,
    expert_slot,
    gate_halves,
    up_halves,
    down_halves,
):
    own_rows = attend(queries, cache_keys, cache_values, new_keys, new_values, lengths)
    attention = lax.all_to_all(own_rows, "tp", split_axis=1, concat_axis=0, tiled=True)
    stream = (residual.astype(jnp.float32) + attention).astype(jnp.bfloat16)
    row_count = stream.shape[0]
    half_rows = row_count // 2
    top_count = routes.shape[1]
    experts = expert_slot.shape[0]
    tp_size = lax.axis_size("tp")
    ep_size = lax.axis_size("ep")
    tp_rank = lax.axis_index("tp")
    width_part = stream.shape[1]
    full_width = width_part * tp_size
    capacity = min(half_rows, 2 * half_rows * top_count // experts)
    gate_local = gate_halves[0]
    up_local = up_halves[0]
    down_local = down_halves[0]
    partials = []
    stream_f = stream.astype(jnp.float32)
    squares = lax.psum(jnp.sum(stream_f * stream_f, axis=1), "tp")
    gain_part = lax.dynamic_slice_in_dim(norm_gain, tp_rank * width_part, width_part).astype(
        jnp.float32
    )
    scaled = lax.rsqrt(squares / full_width + EPSILON)
    normed = (stream_f * scaled[:, None] * gain_part[None, :]).astype(jnp.bfloat16)
    gate_split = gate_local.reshape(tp_size, width_part, -1)
    up_split = up_local.reshape(tp_size, width_part, -1)
    down_split = down_local.reshape(-1, tp_size, width_part)
    for batch_index in range(2):
        row_start = batch_index * half_rows
        batch_rows = normed[row_start : row_start + half_rows]
        select, weighted = expert_tables(
            routes[row_start : row_start + half_rows],
            route_weights[row_start : row_start + half_rows],
            expert_slot,
            capacity,
        )
        select = jnp.repeat(select, 2, axis=0).transpose(1, 0, 2)
        weighted = jnp.repeat(weighted, 2, axis=0).transpose(1, 0, 2)
        outgoing = jnp.einsum(
            "cjr,rf->cjf",
            select.astype(jnp.bfloat16),
            batch_rows,
            preferred_element_type=jnp.float32,
        ).astype(jnp.bfloat16)
        arrived = lax.all_to_all(outgoing, ("ep", "tp"), split_axis=1, concat_axis=1, tiled=True)
        item_count = arrived.shape[0]
        blocks = arrived.reshape(item_count, ep_size, tp_size, width_part)
        gate_out = jnp.einsum(
            "cabf,bfh->cah", blocks, gate_split, preferred_element_type=jnp.float32
        )
        up_out = jnp.einsum("cabf,bfh->cah", blocks, up_split, preferred_element_type=jnp.float32)
        hidden = (jax.nn.silu(gate_out) * up_out).astype(jnp.bfloat16)
        result = jnp.einsum(
            "cah,hbf->cabf", hidden, down_split, preferred_element_type=jnp.float32
        ).astype(jnp.bfloat16)
        result = result.reshape(item_count, ep_size * tp_size, width_part)
        returned = lax.all_to_all(result, ("ep", "tp"), split_axis=1, concat_axis=1, tiled=True)
        partials.append(
            jnp.einsum(
                "cjr,cjf->rf",
                weighted,
                returned.astype(jnp.float32),
                precision=lax.Precision.HIGHEST,
            )
        )
    mixture = jnp.concatenate(partials, axis=0)
    return (stream.astype(jnp.float32) + mixture).astype(jnp.bfloat16)


def flip(value):
    return 1 - value


def layer_kernel(
    full_width,
    lengths_ref,
    query_ref,
    key_ref,
    value_ref,
    fresh_key_ref,
    fresh_value_ref,
    residual_ref,
    gain_ref,
    table_ref,
    gate_ref,
    up_ref,
    down_ref,
    out_ref,
    keys,
    values,
    heads_in,
    heads_out,
    att_out,
    att_in,
    stream_ref,
    sq_out,
    sq_in,
    tables,
    rows_all,
    pieces,
    from_mate,
    from_b,
    from_a,
    from_z,
    wide_w,
    down_w,
    acc_ref,
    load_sem,
    att_send,
    att_recv,
    sq_send,
    sq_recv,
    table_send,
    table_z,
    table_y,
    go_send,
    z_recv,
    a_recv,
    b_recv,
    mate_recv,
    back_send,
    back_mate,
    back_b,
    back_a,
    back_z,
):
    ep = lax.axis_index("ep")
    tp = lax.axis_index("tp")
    z, y = ep // 2, ep % 2
    x, c = tp // 2, tp % 2
    hidden_width = gate_ref.shape[1]
    row_count, width = residual_ref.shape
    half_rows = row_count // 2
    own_rows = query_ref.shape[0]
    head_dim = fresh_key_ref.shape[2]
    head_count = query_ref.shape[1] // head_dim
    own_half = own_rows // 2
    kv_heads = fresh_key_ref.shape[1]
    span = key_ref.shape[1] // kv_heads
    group = head_count // kv_heads

    def half_load(source, target, h, index):
        part = pl.ds(h * own_half, own_half)
        return pltpu.make_async_copy(source.at[part], target.at[part], load_sem.at[index])

    cache_loads = [
        [half_load(key_ref, keys, h, 2 * h), half_load(value_ref, values, h, 2 * h + 1)]
        for h in (0, 1)
    ]
    loads = [
        pltpu.make_async_copy(gate_ref, wide_w.at[:, pl.ds(0, hidden_width)], load_sem.at[4]),
        pltpu.make_async_copy(
            up_ref, wide_w.at[:, pl.ds(hidden_width, hidden_width)], load_sem.at[5]
        ),
        pltpu.make_async_copy(down_ref, down_w, load_sem.at[6]),
    ]
    for load in cache_loads[0] + cache_loads[1] + loads:
        load.start()

    z_of = [z, z + 1 - 2 * (z % 2), z + 2 - 4 * (z // 2), 3 - z]
    tp_of = [tp, tp + 1 - 2 * c, tp + 2 - 4 * x, 3 - tp]
    mate = (ep, tp_of[1])
    step_y = 1 - 2 * y
    step_x = 2 - 4 * x
    peer_y = (ep + step_y, tp)
    peer_a = (ep + (1 - c) * step_y, tp + c * step_x)
    peer_b = (ep + c * step_y, tp + (1 - c) * step_x)
    peer_z = [None] + [(2 * z_of[k] + y, tp) for k in (1, 2, 3)]
    own_a = y * (1 - c) + x * c
    own_b = x * (1 - c) + y * c

    def to(device):
        return {"ep": device[0], "tp": device[1]}

    barrier = pltpu.get_barrier_semaphore()
    greeted = [mate, peer_a, peer_b, (ep, tp_of[3])] + peer_z[1:]
    for device in greeted:
        pl.semaphore_signal(
            barrier, inc=1, device_id=to(device), device_id_type=pl.DeviceIdType.MESH
        )

    sent = []

    def push(source, target, send_sem, recv_sem, device):
        copy = pltpu.make_async_remote_copy(
            src_ref=source,
            dst_ref=target,
            send_sem=send_sem,
            recv_sem=recv_sem,
            device_id=to(device),
            device_id_type=pl.DeviceIdType.MESH,
        )
        copy.start()
        sent.append(copy)

    def arrived(target, recv_sem, device):
        pltpu.make_async_remote_copy(
            src_ref=target,
            dst_ref=target,
            send_sem=recv_sem,
            recv_sem=recv_sem,
            device_id=to(device),
            device_id_type=pl.DeviceIdType.MESH,
        ).wait_recv()

    def columns(index):
        return pl.ds(pl.multiple_of(index * width, width), width)

    score_scale = 1.0 / float(head_dim) ** 0.5
    head_at = lax.broadcasted_iota(jnp.int32, (head_count, kv_heads * span), 0)
    key_at = lax.broadcasted_iota(jnp.int32, (head_count, kv_heads * span), 1)
    same_group = head_at // group == key_at // span
    position = jnp.where(same_group, key_at % span, span)

    def per_head(value):
        return jnp.concatenate(
            [jnp.broadcast_to(value[g : g + 1], (group, head_dim)) for g in range(kv_heads)], axis=0
        )

    def attend_row(row, at):
        query = heads_in[at].astype(jnp.bfloat16)
        scores = lax.dot_general(
            query, keys[row], (((1,), (1,)), ((), ())), preferred_element_type=jnp.float32
        )
        scores = jnp.where(position < lengths_ref[row], scores * score_scale, -1e30)
        fresh_key = per_head(fresh_key_ref[row].astype(jnp.float32))
        fresh = (
            jnp.sum(query.astype(jnp.float32) * fresh_key, axis=1, keepdims=True) * score_scale
        )
        top = jnp.maximum(jnp.max(scores, axis=1, keepdims=True), fresh)
        weights = jnp.exp(scores - top)
        fresh_weight = jnp.exp(fresh - top)
        total = jnp.sum(weights, axis=1, keepdims=True) + fresh_weight
        mixed = jnp.dot(
            weights.astype(jnp.bfloat16), values[row], preferred_element_type=jnp.float32
        )
        mixed = mixed + fresh_weight * per_head(fresh_value_ref[row].astype(jnp.float32))
        heads_out[at] = mixed / total

    def attend_half(h):
        for load in cache_loads[h]:
            load.wait()

        def some_rows(i, carry):
            for u in range(UNROLL):
                attend_row(h * own_half + i * UNROLL + u, i * UNROLL + u)
            return carry

        per_part = head_count // 4
        for t in range(4):
            part = query_ref[h * own_half : (h + 1) * own_half, t * width : (t + 1) * width]
            heads_in[:, t * per_part : (t + 1) * per_part, :] = part.astype(jnp.float32).reshape(
                own_half, per_part, head_dim
            )
        lax.fori_loop(0, own_half // UNROLL, some_rows, 0)
        for t in range(4):
            part = heads_out[:, t * per_part : (t + 1) * per_part, :]
            att_out[h, t] = part.reshape(own_half, width).astype(jnp.bfloat16)

    def send_attention(h):
        for d in (3, 2, 1):
            push(
                att_out.at[h, tp_of[d]],
                att_in.at[h, tp],
                att_send.at[4 * h + d],
                att_recv.at[4 * h + d],
                (ep, tp_of[d]),
            )
        att_in[h, tp] = att_out[h, tp]

    def own_squares(h):
        for d in (1, 2, 3):
            arrived(att_in.at[h, tp_of[d]], att_recv.at[4 * h + d], (ep, tp_of[d]))
        residual = jnp.concatenate(
            [
                residual_ref[(2 * t + h) * own_half : (2 * t + h + 1) * own_half]
                for t in range(4)
            ],
            axis=0,
        )
        attention = att_in[h].reshape(half_rows, width)
        stream = (residual.astype(jnp.float32) + attention.astype(jnp.float32)).astype(
            jnp.bfloat16
        )
        stream_ref[h] = stream
        stream_f = stream.astype(jnp.float32)
        rows_all[z, y, tp, h * half_rows : (h + 1) * half_rows] = (
            stream_f * gain_ref[:, columns(tp)].astype(jnp.float32)
        ).astype(jnp.bfloat16)
        return jnp.sum(stream_f * stream_f, axis=1, keepdims=True)

    def push_table(k):
        push(
            tables.at[z_of[k], y],
            tables.at[z_of[k], y],
            table_send.at[4 + k],
            table_y.at[k],
            peer_y,
        )

    def place(ra, rb):
        a = own_a if ra == 0 else flip(own_a)
        b = own_b if rb == 0 else flip(own_b)
        return a * (1 - c) + b * c, a * c + b * (1 - c)

    def slot(n, ra, rb):
        y_at, x_at = place(ra, rb)
        return rows_all.at[
            z_of[n // 2], y_at, 2 * x_at + c, pl.ds(n % 2 * half_rows, half_rows)
        ]

    def mate_slot(n, ra, rb):
        y_at, x_at = place(rb, ra)
        return rows_all.at[
            z_of[n // 2], y_at, 2 * x_at + flip(c), pl.ds(n % 2 * half_rows, half_rows)
        ]

    def go(block, index, recv_sem, device):
        push(block, block, go_send.at[index], recv_sem, device)

    def forward(n, ra, rb):
        block = slot(n, ra, rb)
        if (ra, rb) == (0, 0):
            go(block, n * 8, a_recv.at[n], peer_a)
            go(block, n * 8 + 1, b_recv.at[2 * n], peer_b)
        if (ra, rb) == (1, 0):
            go(block, n * 8 + 2, b_recv.at[2 * n + 1], peer_b)
        role = 2 * ra + rb
        go(block, n * 8 + 3 + role, mate_recv.at[4 * n + role], mate)

    def begin(h):
        for k in (1, 2, 3):
            go(slot(h, 0, 0), 64 + 3 * h + k - 1, z_recv.at[2 * k + h], peer_z[k])
        forward(h, 0, 0)

    def take_z(n):
        if n >= 2:
            arrived(slot(n, 0, 0), z_recv.at[n], peer_z[n // 2])
            forward(n, 0, 0)

    def take_a(n):
        arrived(slot(n, 1, 0), a_recv.at[n], peer_a)
        forward(n, 1, 0)

    def take_b(n, ra):
        arrived(slot(n, ra, 1), b_recv.at[2 * n + ra], peer_b)
        forward(n, ra, 1)

    slot_id = (ep * 4 + tp) // 2

    def compute(n):
        k, h = n // 2, n % 2
        z_at = z_of[k]
        for ra in (0, 1):
            for rb in (0, 1):
                arrived(mate_slot(n, ra, rb), mate_recv.at[4 * n + 2 * ra + rb], mate)
        if n == 0:
            for load in loads:
                load.wait()
        if h == 0:
            arrived(tables.at[z_at, flip(y)], table_y.at[k], peer_y)
        span_rows = pl.ds(h * half_rows, half_rows)
        acc_ref[...] = jnp.zeros_like(acc_ref)

        def add_part(t, carry):
            acc_ref[...] += jnp.dot(
                rows_all[z_at, :, t, span_rows].reshape(row_count, width),
                wide_w[columns(t), :],
                preferred_element_type=jnp.float32,
            )
            return carry

        lax.fori_loop(0, 4, add_part, 0)
        weights = []
        scales = []
        for y_at in (0, 1):
            table = tables[z_at, y_at]
            lines = lax.broadcasted_iota(jnp.int32, table.shape, 0)
            line = jnp.sum(jnp.where(lines == slot_id, table, 0.0), axis=0, keepdims=True)
            weights.append(
                jnp.broadcast_to(line, (row_count, row_count)).T[
                    h * half_rows : (h + 1) * half_rows, 0:1
                ]
            )
            line = table[table.shape[0] - 8 : table.shape[0] - 7]
            scales.append(
                jnp.broadcast_to(line, (row_count, row_count)).T[
                    h * half_rows : (h + 1) * half_rows, 0:1
                ]
            )
        weight = jnp.concatenate(weights, axis=0)
        scale = jnp.concatenate(scales, axis=0)
        gate = acc_ref[:, 0:hidden_width] * scale
        up = acc_ref[:, hidden_width : 2 * hidden_width] * scale
        hidden = (gate / (1.0 + jnp.exp(-gate)) * up * weight).astype(jnp.bfloat16)
        for t in range(4):
            part = jnp.dot(
                hidden,
                down_w[:, t * width : (t + 1) * width],
                preferred_element_type=jnp.float32,
            ).astype(jnp.bfloat16)
            pieces[h, t % 2, z_at, :, t // 2] = part.reshape(2, half_rows, width)
        push(
            pieces.at[h, flip(c), z_at],
            from_mate.at[h, z_at],
            back_send.at[8 * n],
            back_mate.at[n],
            mate,
        )

    def back_1(n):
        h, z_at = n % 2, z_of[n // 2]
        arrived(from_mate.at[h, z_at], back_mate.at[n], mate)
        for rb in (1, 0):
            for ra in (1, 0):
                y_at, x_at = place(ra, rb)
                from_mate[h, z_at, y_at, x_at] = (
                    from_mate[h, z_at, y_at, x_at] + pieces[h, c, z_at, y_at, x_at]
                )
                if rb == 1:
                    push(
                        from_mate.at[h, z_at, y_at, x_at],
                        from_b.at[n, ra],
                        back_send.at[8 * n + 1 + ra],
                        back_b.at[2 * n + ra],
                        peer_b,
                    )

    def back_2(n):
        for ra in (1, 0):
            arrived(from_b.at[n, ra], back_b.at[2 * n + ra], peer_b)
            y_at, x_at = place(ra, 0)
            from_b[n, ra] = from_b[n, ra] + from_mate[n % 2, z_of[n // 2], y_at, x_at]
            if ra == 1:
                push(from_b.at[n, 1], from_a.at[n], back_send.at[8 * n + 3], back_a.at[n], peer_a)

    def back_3(n):
        arrived(from_a.at[n], back_a.at[n], peer_a)
        from_a[n] = from_a[n] + from_b[n, 0]
        if n >= 2:
            push(
                from_a.at[n], from_z.at[n], back_send.at[8 * n + 4], back_z.at[n], peer_z[n // 2]
            )

    def finish(h):
        total = stream_ref[h].astype(jnp.float32) + from_a[h].astype(jnp.float32)
        for k in (1, 2, 3):
            n = 2 * k + h
            arrived(from_z.at[n], back_z.at[n], peer_z[k])
            total = total + from_z[n].astype(jnp.float32)
        total = total.astype(jnp.bfloat16)
        for t in range(4):
            out_ref[(2 * t + h) * own_half : (2 * t + h + 1) * own_half] = total[
                t * own_half : (t + 1) * own_half
            ]

    attend_half(0)
    pl.semaphore_wait(barrier, len(greeted))
    send_attention(0)
    attend_half(1)
    send_attention(1)
    squares_0 = own_squares(0)
    begin(0)
    squares_1 = own_squares(1)
    begin(1)
    own_sq = jnp.concatenate([squares_0, squares_1], axis=0)
    sq_out[...] = jnp.broadcast_to(own_sq, (row_count, row_count)).T[0:8, :]
    for d in (3, 2, 1):
        push(sq_out, sq_in.at[d - 1], sq_send.at[d], sq_recv.at[d], (ep, tp_of[d]))

    def spread_tables():
        for d in (1, 2, 3):
            arrived(sq_in.at[d - 1], sq_recv.at[d], (ep, tp_of[d]))
        squares = sq_out[...] + sq_in[0] + sq_in[1] + sq_in[2]
        scaled = lax.rsqrt(squares / full_width + EPSILON)
        tables[z, y] = jnp.concatenate([table_ref[...], scaled], axis=0)
        for k in (1, 2, 3):
            push(tables.at[z, y], tables.at[z, y], table_send.at[k], table_z.at[k], peer_z[k])
        push_table(0)

    def relay_tables():
        for k in (1, 2, 3):
            arrived(tables.at[z_of[k], y], table_z.at[k], peer_z[k])
            push_table(k)

    order = (0, 1, 2, 4, 6, 3, 5, 7)

    def staged(action, step, lag, *more):
        if 0 <= step - lag < len(order):
            action(order[step - lag], *more)

    for step in range(1, len(order) + 6):
        if step == 2:
            spread_tables()
        if step == 4:
            relay_tables()
        staged(take_z, step, 0)
        staged(take_a, step, 1)
        staged(take_b, step, 1, 0)
        staged(take_b, step, 2, 1)
        staged(back_1, step, 4)
        staged(back_2, step, 5)
        staged(back_3, step, 6)
        staged(compute, step, 3)
    for h in (0, 1):
        finish(h)
    for copy in sent:
        copy.wait_send()


def dense_device(
    queries,
    cache_keys,
    cache_values,
    new_keys,
    new_values,
    lengths,
    residual,
    norm_gain,
    routes,
    route_weights,
    expert_slot,
    gate_halves,
    up_halves,
    down_halves,
):
    experts = expert_slot.shape[0]
    row_count, width = residual.shape
    half_rows = row_count // 2
    hidden_width = gate_halves.shape[2]
    full_width = norm_gain.shape[0]
    own_rows, kv_heads, head_dim = new_keys.shape
    head_count = queries.shape[1] // head_dim
    keys_per_row = cache_keys.shape[1] * cache_keys.shape[2]
    chosen = routes[:, :, None] == jnp.arange(experts, dtype=jnp.int32)
    by_expert = jnp.sum(jnp.where(chosen, route_weights[:, :, None], 0.0), axis=1)
    slots = expert_slot[:, None] == jnp.arange(experts, dtype=jnp.int32)[None, :]
    table = jnp.sum(jnp.where(slots[None], by_expert[:, :, None], 0.0), axis=1)
    table = table.reshape(4, 2, own_rows // 2, experts).transpose(3, 1, 0, 2)
    table = table.reshape(experts, row_count)
    block = (row_count, width)
    half = (half_rows, width)
    cache = (own_rows, keys_per_row, head_dim)
    vmem = pl.BlockSpec(memory_space=pltpu.VMEM)
    smem = pl.BlockSpec(memory_space=pltpu.SMEM)
    anywhere = pl.BlockSpec(memory_space=pl.ANY)
    dma = pltpu.SemaphoreType.DMA
    return pl.pallas_call(
        functools.partial(layer_kernel, full_width),
        out_shape=jax.ShapeDtypeStruct(block, jnp.bfloat16),
        in_specs=[smem, vmem, anywhere, anywhere] + [vmem] * 5 + [anywhere] * 3,
        out_specs=vmem,
        scratch_shapes=[
            pltpu.VMEM(cache, jnp.bfloat16),
            pltpu.VMEM(cache, jnp.bfloat16),
            pltpu.VMEM((own_rows // 2, head_count, head_dim), jnp.float32),
            pltpu.VMEM((own_rows // 2, head_count, head_dim), jnp.float32),
            pltpu.VMEM((2, 4, own_rows // 2, width), jnp.bfloat16),
            pltpu.VMEM((2, 4, own_rows // 2, width), jnp.bfloat16),
            pltpu.VMEM((2,) + half, jnp.bfloat16),
            pltpu.VMEM((8, row_count), jnp.float32),
            pltpu.VMEM((3, 8, row_count), jnp.float32),
            pltpu.VMEM((4, 2, experts + 8, row_count), jnp.float32),
            pltpu.VMEM((4, 2, 4) + block, jnp.bfloat16),
            pltpu.VMEM((2, 2, 4, 2, 2) + half, jnp.bfloat16),
            pltpu.VMEM((2, 4, 2, 2) + half, jnp.bfloat16),
            pltpu.VMEM((8, 2) + half, jnp.bfloat16),
            pltpu.VMEM((8,) + half, jnp.bfloat16),
            pltpu.VMEM((8,) + half, jnp.bfloat16),
            pltpu.VMEM((full_width, 2 * hidden_width), jnp.bfloat16),
            pltpu.VMEM((hidden_width, full_width), jnp.bfloat16),
            pltpu.VMEM((row_count, 2 * hidden_width), jnp.float32),
            dma((7,)),
            dma((8,)),
            dma((8,)),
            dma((4,)),
            dma((4,)),
            dma((8,)),
            dma((4,)),
            dma((4,)),
            dma((72,)),
            dma((8,)),
            dma((8,)),
            dma((16,)),
            dma((32,)),
            dma((64,)),
            dma((8,)),
            dma((16,)),
            dma((8,)),
            dma((8,)),
        ],
        compiler_params=pltpu.CompilerParams(
            collective_id=0, has_side_effects=True, vmem_limit_bytes=58 * 1024 * 1024
        ),
    )(
        lengths,
        queries,
        cache_keys.reshape(cache),
        cache_values.reshape(cache),
        new_keys,
        new_values,
        residual,
        norm_gain.reshape(1, full_width),
        table,
        gate_halves[0],
        up_halves[0],
        down_halves[0],
    )


def on_device(*args):
    routes, expert_slot = args[8], args[10]
    half_rows = routes.shape[0] // 2
    capacity = min(half_rows, 2 * half_rows * routes.shape[1] // expert_slot.shape[0])
    grid = (lax.axis_size("ep"), lax.axis_size("tp"))
    if capacity == half_rows and grid == (8, 4) and routes.shape[0] == 128:
        return dense_device(*args)
    return routed_device(*args)


def solution(mesh):
    return jax.shard_map(
        on_device,
        mesh=mesh,
        in_specs=(
            P(("groups", "ep", "tp"), None),
            P(("groups", "ep", "tp"), None, None, None),
            P(("groups", "ep", "tp"), None, None, None),
            P(("groups", "ep", "tp"), None, None),
            P(("groups", "ep", "tp"), None, None),
            P(("groups", "ep", "tp")),
            P(("groups", "ep"), "tp"),
            P(),
            P(("groups", "ep"), None),
            P(("groups", "ep"), None),
            P(),
            P(("ep", "tp"), None, None),
            P(("ep", "tp"), None, None),
            P(("ep", "tp"), None, None),
        ),
        out_specs=P(("groups", "ep"), "tp"),
        check_vma=False,
    )
```
